1024 devices in a mesh: row: 16 (over z, y_hi), col: 64 (over x, y_lo, core).
Axes of the slice: x: 8, y: 8 (y_hi: 2, y_lo: 4; y = y_hi * 4 + y_lo), z: 8, core: 2. Of those that a mesh axis runs over, the one named last changes fastest.
Arguments:
- vectors: float32 [1536, 384, 128], P('row', 'col'), may hold values from -0.02734375 to 0.02734375
- hblocks: float32 [384, 7, 128, 128], P('col'), may hold values from -1 to 1, as said below
- coupling: int32 [384, 6], P('col'), may hold values from 0 to 1, as said below
Outputs:
- projected_ham: float32 [1536, 1536], P('row', 'col')
- intersection: float32 [1536, 1536], P('row', 'col')
The draws below stay inside these ranges and needn't reach their ends.
Inputs may be any that keep to these rules, and one draw needn't show every extreme that they name: For 1 <= k <= 3 and a >= k, hblocks[a, 3 - k] is the transpose of hblocks[a - k, 3 + k], and hblocks[a, 3] is symmetric, so the Hamiltonian is symmetric. coupling[a, 3 + k - 1] equals coupling[a + k, 3 - k] for 1 <= k <= 3; entries that name an atom outside the chain are 0.
All inputs are finite; a program needn't handle non-finite values.
Results may differ from the reference program's by a relative error of at most 0.0001.
Values sent between devices are 32-bit elements; how exact they have to be, the bound alone decides.
A program may use at most 64 MiB of HBM per device.

```python
import jax
import jax.numpy as jnp
from jax import lax

BLOCK = 128
STATES = 1536
REACH = 3
DEGREE = 3
ATOMS = 384
BASIS = 49152


def draw_hblocks(key, part):
    key = jax.random.fold_in(key, 11)
    shape = (ATOMS, REACH + 1, BLOCK, BLOCK)
    raw = jnp.clip(0.3 * jax.random.normal(key, shape, jnp.float32), -1.0, 1.0)
    middle = 0.5 * (raw[:, 0] + jnp.swapaxes(raw[:, 0], -1, -2))
    lefts = []
    rights = []
    for offset in range(1, REACH + 1):
        rights.append(raw[:, offset])
        lefts.append(jnp.swapaxes(jnp.roll(raw[:, offset], offset, axis=0), -1, -2))
    ordered = lefts[::-1] + [middle] + rights
    return jnp.stack(ordered, axis=1)


def draw_coupling(key, part):
    key = jax.random.fold_in(key, 23)
    bonds = (jax.random.randint(key, (ATOMS, REACH), 0, 4) > 0).astype(jnp.int32)
    places = jnp.arange(ATOMS, dtype=jnp.int32)[:, None]
    reach_ids = jnp.arange(1, REACH + 1, dtype=jnp.int32)[None, :]
    bonds = bonds * (places + reach_ids < ATOMS).astype(jnp.int32)
    lefts = []
    for offset in range(1, REACH + 1):
        lefts.append(jnp.roll(bonds[:, offset - 1], offset, axis=0))
    left_part = jnp.stack(lefts[::-1], axis=1)
    return jnp.concatenate([left_part, bonds], axis=1)


def shard_levels(rng, dims, split, low, largest):
    level = 1.0
    for axis_at, parts in split:
        draws = jax.random.uniform(jax.random.fold_in(jax.random.fold_in(rng, 6), axis_at), (parts,), jnp.float32, low / len(split), largest / len(split))
        level = level * jnp.repeat(jnp.exp(draws), dims[axis_at] // parts).reshape((-1,) + (1,) * (len(dims) - 1 - axis_at))
    return level


def gaussian(own_key, extent, deviation, limit, shards=(), held_as=jnp.bfloat16):
    array = jax.random.normal(own_key, extent, jnp.float32) * deviation
    if len(shards) > 0:
        array = shard_levels(own_key, extent, shards, -0.22, 0.18) * array
    return jnp.clip(array, min=-limit, max=limit).astype(held_as)


def setup_inputs(seed: int = 0) -> dict:
    streams_of = jax.random.split(jax.random.key(seed), 4)
    return {
        "vectors": gaussian(streams_of[0], (STATES, ATOMS, BLOCK), BASIS ** -0.5, 0.02734375, ((0, 16), (1, 64)), jnp.float32),
        "hblocks": draw_hblocks(jax.random.fold_in(streams_of[3], 71), 0),
        "coupling": draw_coupling(jax.random.fold_in(streams_of[3], 71), 0),
    }


CENTER = 0.5
HALF_WIDTH = 1.5
HSCALE = 0.1


def masked_blocks(hblocks, coupling):
    ones = jnp.ones((coupling.shape[0], 1), jnp.int32)
    presence = jnp.concatenate([coupling[:, :REACH], ones, coupling[:, REACH:]], axis=1)
    return HSCALE * hblocks * presence.astype(jnp.float32)[:, :, None, None]


def apply_ham(field, blocks):
    atoms = field.shape[1]
    padded = jnp.pad(field, ((0, 0), (REACH, REACH), (0, 0)))
    result = jnp.zeros(field.shape, jnp.float32)
    for offset in range(2 * REACH + 1):
        shifted = padded[:, offset:offset + atoms, :]
        result = result + jnp.einsum("saj,aij->sai", shifted, blocks[:, offset], precision=lax.Precision.HIGHEST)
    return result


def reference(vectors, hblocks, coupling):
    blocks = masked_blocks(hblocks, coupling)
    y_prev = vectors
    y_now = (apply_ham(vectors, blocks) - CENTER * vectors) / HALF_WIDTH
    for section in range(DEGREE - 1):
        y_next = 2.0 * (apply_ham(y_now, blocks) - CENTER * y_now) / HALF_WIDTH - y_prev
        y_prev = y_now
        y_now = y_next
    image = apply_ham(y_now, blocks)
    flat_y = y_now.reshape(y_now.shape[0], -1)
    flat_w = image.reshape(image.shape[0], -1)
    projected_ham = jnp.einsum("sn,tn->st", flat_y, flat_w, precision=lax.Precision.HIGHEST)
    intersection = jnp.einsum("sn,tn->st", flat_y, flat_y, precision=lax.Precision.HIGHEST)
    return (projected_ham, intersection)
```

```python
import functools

import jax
import jax.numpy as jnp
from jax import lax
from jax.experimental import pallas as pl
from jax.experimental.pallas import tpu as pltpu
from jax.sharding import PartitionSpec as P

REACH = 3
DEGREE = 3

CENTER = 0.5
HALF_WIDTH = 1.5
HSCALE = 0.1

LANES = 128
OWN = 6
PAIRS = OWN // 2
WINDOW = 8
MESH = pl.DeviceIdType.MESH


def split_high_low(value):
    high = value.astype(jnp.bfloat16)
    low = (value - high.astype(jnp.float32)).astype(jnp.bfloat16)
    return high, low


def dot_last(left, right):
    return lax.dot_general(
        left, right, (((1,), (1,)), ((), ())), preferred_element_type=jnp.float32
    )


def kernel(
    ring,
    states,
    coupling,
    vectors,
    hblocks,
    out_gram,
    out_ham,
    raw,
    band_high,
    band_low,
    fields,
    halo,
    operand,
    acc,
    image,
    blocks,
    image_block,
    sibling,
    side_high,
    side_low,
    other,
    products,
    parts,
    sums,
    last,
    load_sem,
    halo_send,
    halo_recv,
    swap_send,
    swap_recv,
    sib_send,
    sib_recv,
    ring_send,
    ring_recv,
    first_send,
    first_recv,
    second_send,
    second_recv,
):
    quarter = ring // 2
    half = ring // 2
    line = ring
    rows = states // quarter

    row = lax.axis_index("row")
    col = lax.axis_index("col")
    z, y_hi = row // 2, row % 2
    x = col // (2 * quarter)
    y_lo = (col // 2) % quarter
    core = col % 2
    y = y_hi * quarter + y_lo
    last_col = ring * 2 * quarter - 1

    def device(z_at, y_at, x_at, core_at):
        return (
            z_at * 2 + y_at // quarter,
            x_at * (2 * quarter) + (y_at % quarter) * 2 + core_at,
        )

    has_low, has_high = col > 0, col < last_col
    stays = y_hi == core
    moves = y_hi != core
    my_pos = jnp.where(core == 0, y, x)
    my_other = jnp.where(core == 0, x, y)
    my_half = my_pos // quarter
    my_piece = core * quarter + my_pos % quarter
    my_out = 2 * y_lo + core
    sends_to_self = jnp.logical_and(my_piece == my_out, x % 2 == my_half)

    def line_device(pos):
        return device(z, jnp.where(core == 0, pos, y), jnp.where(core == 0, x, pos), core)

    def owner_device(target, side):
        return device(z, side * quarter + my_piece // 2, target, my_piece % 2)

    src_core = my_out // quarter
    src_pos = (my_out % quarter + quarter * x) % line

    def source_device(at):
        return device(
            z, jnp.where(src_core == 0, src_pos, at), jnp.where(src_core == 0, at, src_pos), src_core
        )

    low_device, high_device = (row, col - 1), (row, col + 1)
    swap_device = device(z, core * quarter + y_lo, x, y_hi)
    sib_device = device(z, y, x, 1 - core)
    down_device = device((z + ring - 1) % ring, y, x, core)
    up_device = device((z + 1) % ring, y, x, core)

    load = pltpu.make_async_copy(hblocks, raw, load_sem.at[0])
    load.start()

    barrier = pltpu.get_barrier_semaphore()

    def greet(target, when=None):
        def signal():
            pl.semaphore_signal(barrier, inc=1, device_id=target, device_id_type=MESH)

        if when is None:
            signal()
        else:
            pl.when(when)(signal)

    greet(low_device, has_low)
    greet(high_device, has_high)
    greet(swap_device, moves)
    greet(sib_device)
    greet(down_device)
    greet(up_device)
    for pos in range(line):
        greet(line_device(pos), my_pos != pos)
    for item in range(half):
        target = 2 * item + my_half
        for side in range(2):
            is_self = sends_to_self & (target == x) & (side == y_hi)
            greet(owner_device(target, side), jnp.logical_not(is_self))
    for at in range(line):
        is_self = sends_to_self & (my_other == at)
        greet(source_device(at), jnp.logical_not(is_self))

    for a in range(OWN):
        fields[0, a] = vectors[:, a, :]

    greetings = (
        has_low.astype(jnp.int32)
        + has_high.astype(jnp.int32)
        + moves.astype(jnp.int32)
        + 3
        + (line - 1)
        + 2 * half
        + line
        - 2 * sends_to_self.astype(jnp.int32)
    )
    pl.semaphore_wait(barrier, greetings)

    unfinished = []

    def remote(src, dst, send, recv, target):
        return pltpu.make_async_remote_copy(
            src_ref=src,
            dst_ref=dst,
            send_sem=send,
            recv_sem=recv,
            device_id=target,
            device_id_type=MESH,
        )

    def start(copy, when=None):
        if when is None:
            copy.start()
            unfinished.append(copy.wait_send)
        else:
            pl.when(when)(copy.start)
            unfinished.append(lambda: pl.when(when)(copy.wait_send))

    def halo_copy(step, side):
        if side == 0:
            src, target = fields.at[step, pl.ds(OWN - REACH, REACH)], high_device
        else:
            src, target = fields.at[step, pl.ds(0, REACH)], low_device
        return remote(
            src, halo.at[step, side], halo_send.at[step, side], halo_recv.at[step, side], target
        )

    def send_halo(step):
        start(halo_copy(step, 0), has_high)
        start(halo_copy(step, 1), has_low)

    send_halo(0)

    load.wait()
    zero_block = jnp.zeros((LANES, LANES), jnp.bfloat16)
    for p in range(PAIRS):
        for band in (band_high, band_low):
            band[p, pl.ds(0, LANES), pl.ds((WINDOW - 1) * LANES, LANES)] = zero_block
            band[p, pl.ds(LANES, LANES), pl.ds(0, LANES)] = zero_block
        for second in range(2):
            a = 2 * p + second
            for o in range(2 * REACH + 1):
                scaled = HSCALE * raw[a, o]
                if o != REACH:
                    bond = coupling[a, o if o < REACH else o - 1]
                    scaled = scaled * bond.astype(jnp.float32)
                high, low = split_high_low(scaled)
                at = (pl.ds(second * LANES, LANES), pl.ds((o + second) * LANES, LANES))
                band_high[(p,) + at] = high
                band_low[(p,) + at] = low

    def put_operand(where, value):
        high, low = split_high_low(value)
        operand[pl.ds(0, states), pl.ds(where * LANES, LANES)] = high
        operand[pl.ds(states, states), pl.ds(where * LANES, LANES)] = low

    def band_product(p, begin, end):
        both = dot_last(
            operand[:, begin * LANES : end * LANES],
            band_high[p, :, (begin - 2 * p) * LANES : (end - 2 * p) * LANES],
        )
        rest = dot_last(
            operand[:states, begin * LANES : end * LANES],
            band_low[p, :, (begin - 2 * p) * LANES : (end - 2 * p) * LANES],
        )
        return both[:states] + both[states:] + rest

    def clear_edge(begin):
        operand[:, pl.ds(begin * LANES, REACH * LANES)] = jnp.zeros(
            (2 * states, REACH * LANES), jnp.bfloat16
        )

    pl.when(jnp.logical_not(has_low))(lambda: clear_edge(0))
    pl.when(jnp.logical_not(has_high))(lambda: clear_edge(REACH + OWN))

    def apply_own(step):
        for a in range(OWN):
            put_operand(REACH + a, fields[step, a])
        for p in range(PAIRS):
            begin, end = max(REACH, 2 * p), min(REACH + OWN, 2 * p + WINDOW)
            acc[p] = band_product(p, begin, end)

    def apply_halo(step):
        def take(side, begin):
            halo_copy(step, side).wait_recv()
            for a in range(REACH):
                put_operand(begin + a, halo[step, side, a])

        pl.when(has_low)(lambda: take(0, 0))
        for p in range(PAIRS):
            if 2 * p < REACH:
                acc[p] = acc[p] + band_product(p, 2 * p, REACH)
        pl.when(has_high)(lambda: take(1, REACH + OWN))
        for p in range(PAIRS):
            if 2 * p + WINDOW > REACH + OWN:
                acc[p] = acc[p] + band_product(p, REACH + OWN, 2 * p + WINDOW)

    def acted(a):
        return acc[a // 2, :, pl.ds((a % 2) * LANES, LANES)]

    for step in range(DEGREE):
        apply_own(step)
        apply_halo(step)
        for a in range(OWN):
            now = fields[step, a]
            if step == 0:
                fields[1, a] = (acted(a) - CENTER * now) / HALF_WIDTH
            else:
                fields[step + 1, a] = (
                    2.0 * (acted(a) - CENTER * now) / HALF_WIDTH - fields[step - 1, a]
                )
        send_halo(step + 1)

    def ring_copy(slot, chunk):
        part = pl.ds(chunk * REACH, REACH)
        upward = slot > half or (slot == half and chunk == 1)
        src, target = ((slot + 1) % ring, up_device) if upward else (slot - 1, down_device)
        return remote(
            blocks.at[src, part],
            blocks.at[slot, part],
            ring_send.at[slot, chunk],
            ring_recv.at[slot, chunk],
            target,
        )

    def ring_pieces(distance):
        if distance == half:
            return [(half, 0), (half, 1)]
        return [(slot, chunk) for chunk in range(2) for slot in (distance, ring - distance)]

    def swap_copy(at):
        src, dst = ((fields.at[DEGREE], blocks.at[0]), (image, image_block))[at]
        return remote(src, dst, swap_send.at[at], swap_recv.at[at], swap_device)

    def sib_copy(at):
        src = (blocks.at[0], image_block)[at]
        return remote(src, sibling.at[at], sib_send.at[at], sib_recv.at[at], sib_device)

    def keep_field():
        blocks[0] = fields[DEGREE]
        for piece in ring_pieces(1):
            ring_copy(*piece).start()

    def keep_image():
        image_block[...] = image[...]

    def take_field():
        swap_copy(0).wait_recv()
        for piece in ring_pieces(1):
            ring_copy(*piece).start()

    start(swap_copy(0), moves)
    pl.when(stays)(keep_field)
    for piece in ring_pieces(1):
        unfinished.append(ring_copy(*piece).wait_send)

    apply_own(DEGREE)
    apply_halo(DEGREE)
    for a in range(OWN):
        image[a] = acted(a)
    start(swap_copy(1), moves)
    pl.when(stays)(keep_image)
    pl.when(moves)(take_field)
    start(sib_copy(0))

    def forward(distance):
        for slot, chunk in ring_pieces(distance):
            ring_copy(slot, chunk).wait_recv()
            if distance < half:
                beyond = slot + 1 if slot < half else slot - 1
                if beyond != half or chunk == (0 if slot < half else 1):
                    start(ring_copy(beyond, chunk))

    def put_side(begin, source):
        for a in range(OWN):
            high, low = split_high_low(source(a))
            at = (pl.ds(begin, states), pl.ds(a * LANES, LANES))
            side_high[at] = high
            side_low[at] = low

    own_rows = pl.multiple_of(core * (2 * states), 2 * states)
    sib_rows = pl.multiple_of((1 - core) * (2 * states), 2 * states)
    put_side(own_rows, lambda a: blocks[0, a])

    forward(1)

    pl.when(moves)(swap_copy(1).wait_recv)
    start(sib_copy(1))
    put_side(own_rows + states, lambda a: image_block[a])
    sib_copy(0).wait_recv()
    put_side(sib_rows, lambda a: sibling[0, a])
    sib_copy(1).wait_recv()
    put_side(sib_rows + states, lambda a: sibling[1, a])

    def first_copy(slot, piece):
        target = (z + slot) % ring
        pos = (piece + quarter * target) % line
        copy = remote(
            products.at[slot, pl.ds(piece * rows, rows)],
            parts.at[target // 2, my_pos],
            first_send.at[slot, piece],
            first_recv.at[target // 2, my_pos],
            line_device(pos),
        )
        return copy, pos, target // 2

    def multiply(slot):
        for a in range(OWN):
            high, low = split_high_low(blocks[slot, a])
            other[pl.ds(0, states), pl.ds(a * LANES, LANES)] = high
            other[pl.ds(states, states), pl.ds(a * LANES, LANES)] = low
        both = dot_last(other[...], side_high[...])
        rest = dot_last(other[:states], side_low[...])
        products[slot] = both[:states] + both[states:] + rest
        for piece in range(quarter):
            copy, pos, item = first_copy(slot, piece)

            def keep(item=item, piece=piece):
                parts[item, my_pos] = products[slot, pl.ds(piece * rows, rows), :]

            start(copy, pos != my_pos)
            pl.when(pos == my_pos)(keep)

    multiply(0)
    for distance in range(1, half + 1):
        if distance > 1:
            forward(distance)
        multiply(distance)
        if distance != half:
            multiply(ring - distance)

    order = sorted(range(ring), key=lambda d: (min(d, ring - d), d))
    even = [d for d in order if d % 2 == 0]
    odd = [d for d in order if d % 2 == 1]
    parity = (z + my_half) % 2
    spans = []
    for side in range(2):
        begin = side * 2 * states // LANES * LANES
        end = -(-(side + 1) * 2 * states // LANES) * LANES
        spans.append((begin, end))

    def second_copy(item, side, target):
        begin, end = spans[side]
        return remote(
            sums.at[item, :, pl.ds(begin, end - begin)],
            last.at[my_other],
            second_send.at[item, side],
            second_recv.at[my_other],
            owner_device(target, side),
        )

    for at in range(half):
        slot = jnp.where(parity == 0, even[at], odd[at])
        target = (z + slot) % ring
        item = target // 2
        for pos in range(line):
            arrival = remote(
                parts.at[item, pos],
                parts.at[item, pos],
                first_send.at[0, 0],
                first_recv.at[item, pos],
                line_device(pos),
            )
            pl.when(my_pos != pos)(arrival.wait_recv)
        total = parts[item, 0]
        for pos in range(1, line):
            total = total + parts[item, pos]
        sums[item] = total
        for side in range(2):
            begin, end = spans[side]
            is_self = sends_to_self & (target == x) & (side == y_hi)

            def keep_sum(item=item, begin=begin, end=end):
                last[my_other] = sums[item, :, pl.ds(begin, end - begin)]

            start(second_copy(item, side, target), jnp.logical_not(is_self))
            pl.when(is_self)(keep_sum)

    for at in range(line):
        is_self = sends_to_self & (my_other == at)
        arrival = remote(
            last.at[at], last.at[at], second_send.at[0, 0], second_recv.at[at], source_device(at)
        )
        pl.when(jnp.logical_not(is_self))(arrival.wait_recv)
    total = last[0]
    for at in range(1, line):
        total = total + last[at]
    skip = 2 * states - spans[1][0]
    gram = jnp.where(y_hi == 0, total[:, :states], total[:, skip : skip + states])
    ham = jnp.where(
        y_hi == 0, total[:, states : 2 * states], total[:, skip + states : skip + 2 * states]
    )
    out_gram[...] = gram
    out_ham[...] = ham

    for finish in unfinished:
        finish()


def per_device(ring, vectors, hblocks, coupling):
    states = vectors.shape[0]
    quarter, half, line = ring // 2, ring // 2, ring
    rows = states // quarter
    width = -(-2 * states // LANES) * LANES
    f32, bf16 = jnp.float32, jnp.bfloat16
    dma = pltpu.SemaphoreType.DMA
    gram, ham = pl.pallas_call(
        functools.partial(kernel, ring, states),
        out_shape=[jax.ShapeDtypeStruct((rows, states), f32)] * 2,
        in_specs=[
            pl.BlockSpec(memory_space=pltpu.SMEM),
            pl.BlockSpec(memory_space=pltpu.VMEM),
            pl.BlockSpec(memory_space=pl.ANY),
        ],
        out_specs=[pl.BlockSpec(memory_space=pltpu.VMEM)] * 2,
        scratch_shapes=[
            pltpu.VMEM((OWN, 2 * REACH + 1, LANES, LANES), f32),
            pltpu.VMEM((PAIRS, 2 * LANES, WINDOW * LANES), bf16),
            pltpu.VMEM((PAIRS, 2 * LANES, WINDOW * LANES), bf16),
            pltpu.VMEM((DEGREE + 1, OWN, states, LANES), f32),
            pltpu.VMEM((DEGREE + 1, 2, REACH, states, LANES), f32),
            pltpu.VMEM((2 * states, (OWN + 2 * REACH) * LANES), bf16),
            pltpu.VMEM((PAIRS, states, 2 * LANES), f32),
            pltpu.VMEM((OWN, states, LANES), f32),
            pltpu.VMEM((ring, OWN, states, LANES), f32),
            pltpu.VMEM((OWN, states, LANES), f32),
            pltpu.VMEM((2, OWN, states, LANES), f32),
            pltpu.VMEM((4 * states, OWN * LANES), bf16),
            pltpu.VMEM((4 * states, OWN * LANES), bf16),
            pltpu.VMEM((2 * states, OWN * LANES), bf16),
            pltpu.VMEM((ring, states, 4 * states), f32),
            pltpu.VMEM((half, line, rows, 4 * states), f32),
            pltpu.VMEM((half, rows, 4 * states), f32),
            pltpu.VMEM((line, rows, width), f32),
            dma((1,)),
            dma((DEGREE + 1, 2)),
            dma((DEGREE + 1, 2)),
            dma((2,)),
            dma((2,)),
            dma((2,)),
            dma((2,)),
            dma((ring, 2)),
            dma((ring, 2)),
            dma((ring, quarter)),
            dma((half, line)),
            dma((half, 2)),
            dma((line,)),
        ],
        compiler_params=pltpu.CompilerParams(
            collective_id=0, has_side_effects=True, vmem_limit_bytes=48 * 1024 * 1024
        ),
    )(coupling, vectors, hblocks)
    return ham.T, gram.T


def solution(mesh):
    in_specs = (P("row", "col", None), P("col", None, None, None), P("col", None))
    out_specs = (P("row", "col"), P("row", "col"))
    ring = mesh.shape["row"] // 2
    return jax.shard_map(
        functools.partial(per_device, ring),
        mesh=mesh,
        in_specs=in_specs,
        out_specs=out_specs,
        check_vma=False,
    )
```

```python
import functools

import jax
import jax.numpy as jnp
from jax import lax
from jax.experimental import pallas as pl
from jax.experimental.pallas import tpu as pltpu
from jax.sharding import PartitionSpec as P

REACH = 3
DEGREE = 3

CENTER = 0.5
HALF_WIDTH = 1.5
HSCALE = 0.1

LANES = 128
OWN = 6
PAIRS = OWN // 2
WINDOW = 8
GROUPS = 2
MESH = pl.DeviceIdType.MESH


def split_high_low(value):
    high = value.astype(jnp.bfloat16)
    low = (value - high.astype(jnp.float32)).astype(jnp.bfloat16)
    return high, low


def dot_last(left, right):
    return lax.dot_general(
        left, right, (((1,), (1,)), ((), ())), preferred_element_type=jnp.float32
    )


def kernel(
    ring,
    states,
    coupling,
    vectors,
    hblocks,
    out_gram,
    out_ham,
    bonds,
    raw,
    band_high,
    band_low,
    fields,
    halo,
    operand,
    acc,
    image,
    blocks,
    image_block,
    sibling,
    side_high,
    side_low,
    other,
    products,
    parts,
    sums,
    last,
    load_sem,
    halo_send,
    halo_recv,
    swap_send,
    swap_recv,
    sib_send,
    sib_recv,
    ring_send,
    ring_recv,
    first_send,
    first_recv,
    second_send,
    second_recv,
):
    quarter = ring // 2
    half = ring // 2
    line = ring
    rows = states // quarter
    part = states // GROUPS

    row = lax.axis_index("row")
    col = lax.axis_index("col")
    z, y_hi = row // 2, row % 2
    x = col // (2 * quarter)
    y_lo = (col // 2) % quarter
    core = col % 2
    y = y_hi * quarter + y_lo
    last_col = ring * 2 * quarter - 1

    def device(z_at, y_at, x_at, core_at):
        return (
            z_at * 2 + y_at // quarter,
            x_at * (2 * quarter) + (y_at % quarter) * 2 + core_at,
        )

    has_low, has_high = col > 0, col < last_col
    stays = y_hi == core
    moves = y_hi != core
    my_pos = jnp.where(core == 0, y, x)
    my_other = jnp.where(core == 0, x, y)
    my_half = my_pos // quarter
    my_piece = core * quarter + my_pos % quarter
    my_out = 2 * y_lo + core
    sends_to_self = jnp.logical_and(my_piece == my_out, x % 2 == my_half)

    def line_device(pos):
        return device(z, jnp.where(core == 0, pos, y), jnp.where(core == 0, x, pos), core)

    def owner_device(target, side):
        return device(z, side * quarter + my_piece // 2, target, my_piece % 2)

    src_core = my_out // quarter
    src_pos = (my_out % quarter + quarter * x) % line

    def source_device(at):
        return device(
            z, jnp.where(src_core == 0, src_pos, at), jnp.where(src_core == 0, at, src_pos), src_core
        )

    low_device, high_device = (row, col - 1), (row, col + 1)
    swap_device = device(z, core * quarter + y_lo, x, y_hi)
    sib_device = device(z, y, x, 1 - core)
    down_device = device((z + ring - 1) % ring, y, x, core)
    up_device = device((z + 1) % ring, y, x, core)

    load = pltpu.make_async_copy(hblocks, raw, load_sem.at[0])
    load_field = pltpu.make_async_copy(vectors, fields.at[0], load_sem.at[1])
    load_bonds = pltpu.make_async_copy(coupling, bonds, load_sem.at[2])
    load_field.start()
    load_bonds.start()
    load.start()

    barrier = pltpu.get_barrier_semaphore()

    def greet(target, when=None):
        def signal():
            pl.semaphore_signal(barrier, inc=1, device_id=target, device_id_type=MESH)

        if when is None:
            signal()
        else:
            pl.when(when)(signal)

    greet(low_device, has_low)
    greet(high_device, has_high)
    greet(swap_device, moves)
    greet(sib_device)
    greet(down_device)
    greet(up_device)
    for pos in range(line):
        greet(line_device(pos), my_pos != pos)
    for item in range(half):
        target = 2 * item + my_half
        for side in range(2):
            is_self = sends_to_self & (target == x) & (side == y_hi)
            greet(owner_device(target, side), jnp.logical_not(is_self))
    for at in range(line):
        is_self = sends_to_self & (my_other == at)
        greet(source_device(at), jnp.logical_not(is_self))

    greetings = (
        has_low.astype(jnp.int32)
        + has_high.astype(jnp.int32)
        + moves.astype(jnp.int32)
        + 3
        + (line - 1)
        + 2 * half
        + line
        - 2 * sends_to_self.astype(jnp.int32)
    )
    load_field.wait()
    pl.semaphore_wait(barrier, greetings)

    unfinished = []

    def remote(src, dst, send, recv, target):
        return pltpu.make_async_remote_copy(
            src_ref=src,
            dst_ref=dst,
            send_sem=send,
            recv_sem=recv,
            device_id=target,
            device_id_type=MESH,
        )

    def start(copy, when=None):
        if when is None:
            copy.start()
            unfinished.append(copy.wait_send)
        else:
            pl.when(when)(copy.start)
            unfinished.append(lambda: pl.when(when)(copy.wait_send))

    def group_rows(g):
        return pl.ds(g * part, part)

    def halo_copy(step, side, g):
        first, target = (OWN - REACH, high_device) if side == 0 else (0, low_device)
        return remote(
            fields.at[step, pl.ds(first, REACH), group_rows(g)],
            halo.at[step, side, :, group_rows(g)],
            halo_send.at[step, side, g],
            halo_recv.at[step, side, g],
            target,
        )

    def send_halo(step, g):
        start(halo_copy(step, 0, g), has_high)
        start(halo_copy(step, 1, g), has_low)

    for g in range(GROUPS):
        send_halo(0, g)

    load_bonds.wait()
    load.wait()
    zero_block = jnp.zeros((LANES, LANES), jnp.bfloat16)
    for p in range(PAIRS):
        for band in (band_high, band_low):
            band[p, pl.ds(0, LANES), pl.ds((WINDOW - 1) * LANES, LANES)] = zero_block
            band[p, pl.ds(LANES, LANES), pl.ds(0, LANES)] = zero_block
        for second in range(2):
            a = 2 * p + second
            for o in range(2 * REACH + 1):
                scaled = HSCALE * raw[a, o]
                if o != REACH:
                    bond = bonds[a, o if o < REACH else o - 1]
                    scaled = scaled * bond.astype(jnp.float32)
                high, low = split_high_low(scaled)
                at = (pl.ds(second * LANES, LANES), pl.ds((o + second) * LANES, LANES))
                band_high[(p,) + at] = high
                band_low[(p,) + at] = low

    def put_operand(g, where, value):
        high, low = split_high_low(value)
        operand[pl.ds(2 * g * part, part), pl.ds(where * LANES, LANES)] = high
        operand[pl.ds((2 * g + 1) * part, part), pl.ds(where * LANES, LANES)] = low

    def band_product(g, p, begin, end):
        begin_row, columns = 2 * g * part, slice(begin * LANES, end * LANES)
        window = slice((begin - 2 * p) * LANES, (end - 2 * p) * LANES)
        both = dot_last(
            operand[begin_row : begin_row + 2 * part, columns], band_high[p, :, window]
        )
        rest = dot_last(operand[begin_row : begin_row + part, columns], band_low[p, :, window])
        return both[:part] + both[part:] + rest

    def clear_edge(begin):
        operand[:, pl.ds(begin * LANES, REACH * LANES)] = jnp.zeros(
            (2 * states, REACH * LANES), jnp.bfloat16
        )

    pl.when(jnp.logical_not(has_low))(lambda: clear_edge(0))
    pl.when(jnp.logical_not(has_high))(lambda: clear_edge(REACH + OWN))

    def apply_own(step, g):
        for a in range(OWN):
            put_operand(g, REACH + a, fields[step, a, group_rows(g)])
        for p in range(PAIRS):
            begin, end = max(REACH, 2 * p), min(REACH + OWN, 2 * p + WINDOW)
            acc[p, group_rows(g)] = band_product(g, p, begin, end)

    def apply_halo(step, g):
        def take(side, begin):
            halo_copy(step, side, g).wait_recv()
            for a in range(REACH):
                put_operand(g, begin + a, halo[step, side, a, group_rows(g)])

        pl.when(has_low)(lambda: take(0, 0))
        pl.when(has_high)(lambda: take(1, REACH + OWN))
        for p in range(PAIRS):
            total = acc[p, group_rows(g)]
            if 2 * p < REACH:
                total = total + band_product(g, p, 2 * p, REACH)
            if 2 * p + WINDOW > REACH + OWN:
                total = total + band_product(g, p, REACH + OWN, 2 * p + WINDOW)
            acc[p, group_rows(g)] = total

    def acted(g, a):
        return acc[a // 2, group_rows(g), pl.ds((a % 2) * LANES, LANES)]

    def ring_copy(slot, chunk):
        upward = slot > half or (slot == half and chunk == 1)
        src, target = ((slot + 1) % ring, up_device) if upward else (slot - 1, down_device)
        return remote(
            blocks.at[src, :, group_rows(chunk)],
            blocks.at[slot, :, group_rows(chunk)],
            ring_send.at[slot, chunk],
            ring_recv.at[slot, chunk],
            target,
        )

    def ring_pieces(distance):
        if distance == half:
            return [(half, 0), (half, 1)]
        return [(slot, chunk) for chunk in range(2) for slot in (distance, ring - distance)]

    def swap_copy(at, g):
        src, dst = ((fields.at[DEGREE], blocks.at[0]), (image, image_block))[at]
        return remote(
            src.at[:, group_rows(g)],
            dst.at[:, group_rows(g)],
            swap_send.at[at, g],
            swap_recv.at[at, g],
            swap_device,
        )

    def sib_copy(at, g):
        src = (blocks.at[0], image_block)[at]
        return remote(
            src.at[:, group_rows(g)],
            sibling.at[at, :, group_rows(g)],
            sib_send.at[at, g],
            sib_recv.at[at, g],
            sib_device,
        )

    def forward(distance):
        for slot, chunk in ring_pieces(distance):
            ring_copy(slot, chunk).wait_recv()
            if distance < half:
                beyond = slot + 1 if slot < half else slot - 1
                if beyond != half or chunk == (0 if slot < half else 1):
                    ring_copy(beyond, chunk).start()

    def begin_ring(g):
        for slot, chunk in ring_pieces(1):
            if chunk == g:
                ring_copy(slot, chunk).start()
        sib_copy(0, g).start()

    for distance in range(1, half + 1):
        for piece in ring_pieces(distance):
            unfinished.append(ring_copy(*piece).wait_send)
    for at in range(2):
        for g in range(GROUPS):
            unfinished.append(sib_copy(at, g).wait_send)

    def keep_field(g):
        blocks[0, :, group_rows(g)] = fields[DEGREE, :, group_rows(g)]
        begin_ring(g)

    def take_field():
        for g in range(GROUPS):
            swap_copy(0, g).wait_recv()
            begin_ring(g)

    def keep_image(g):
        image_block[:, group_rows(g)] = image[:, group_rows(g)]
        sib_copy(1, g).start()

    def take_image():
        for g in range(GROUPS):
            swap_copy(1, g).wait_recv()
            sib_copy(1, g).start()

    def put_side(begin, source):
        for a in range(OWN):
            high, low = split_high_low(source(a))
            at = (pl.ds(begin, states), pl.ds(a * LANES, LANES))
            side_high[at] = high
            side_low[at] = low

    own_rows = pl.multiple_of(core * (2 * states), 2 * states)
    sib_rows = pl.multiple_of((1 - core) * (2 * states), 2 * states)

    for step in range(DEGREE):
        for g in range(GROUPS):
            apply_own(step, g)
            apply_halo(step, g)
            for a in range(OWN):
                now = fields[step, a, group_rows(g)]
                if step == 0:
                    later = (acted(g, a) - CENTER * now) / HALF_WIDTH
                else:
                    before = fields[step - 1, a, group_rows(g)]
                    later = 2.0 * (acted(g, a) - CENTER * now) / HALF_WIDTH - before
                fields[step + 1, a, group_rows(g)] = later
            send_halo(step + 1, g)
            if step == DEGREE - 1:
                start(swap_copy(0, g), moves)
                pl.when(stays)(functools.partial(keep_field, g))

    for g in range(GROUPS):
        apply_own(DEGREE, g)
        apply_halo(DEGREE, g)
        for a in range(OWN):
            image[a, group_rows(g)] = acted(g, a)
        start(swap_copy(1, g), moves)
        pl.when(stays)(functools.partial(keep_image, g))
        if g == 0:
            pl.when(stays)(lambda: forward(1))
    pl.when(moves)(take_field)
    if half > 1:
        pl.when(stays)(lambda: forward(2))
    put_side(own_rows, lambda a: blocks[0, a])
    for g in range(GROUPS):
        sib_copy(0, g).wait_recv()
    put_side(sib_rows, lambda a: sibling[0, a])
    pl.when(moves)(lambda: forward(1))
    pl.when(moves)(take_image)
    for distance in range(3, half + 1):
        pl.when(stays)(functools.partial(forward, distance))
    put_side(own_rows + states, lambda a: image_block[a])
    for g in range(GROUPS):
        sib_copy(1, g).wait_recv()
    put_side(sib_rows + states, lambda a: sibling[1, a])

    def first_copy(slot, piece):
        target = (z + slot) % ring
        pos = (piece + quarter * target) % line
        copy = remote(
            products.at[slot, pl.ds(piece * rows, rows)],
            parts.at[target // 2, my_pos],
            first_send.at[slot, piece],
            first_recv.at[target // 2, my_pos],
            line_device(pos),
        )
        return copy, pos, target // 2

    def multiply(slot):
        for a in range(OWN):
            high, low = split_high_low(blocks[slot, a])
            other[pl.ds(0, states), pl.ds(a * LANES, LANES)] = high
            other[pl.ds(states, states), pl.ds(a * LANES, LANES)] = low
        both = dot_last(other[...], side_high[...])
        rest = dot_last(other[:states], side_low[...])
        products[slot] = both[:states] + both[states:] + rest
        for piece in range(quarter):
            copy, pos, item = first_copy(slot, piece)

            def keep(item=item, piece=piece):
                parts[item, my_pos] = products[slot, pl.ds(piece * rows, rows), :]

            start(copy, pos != my_pos)
            pl.when(pos == my_pos)(keep)

    multiply(0)
    for distance in range(1, half + 1):
        if distance > 1:
            pl.when(moves)(functools.partial(forward, distance))
        multiply(distance)
        if distance != half:
            multiply(ring - distance)

    order = sorted(range(ring), key=lambda d: (min(d, ring - d), d))
    even = [d for d in order if d % 2 == 0]
    odd = [d for d in order if d % 2 == 1]
    parity = (z + my_half) % 2
    spans = []
    for side in range(2):
        begin = side * 2 * states // LANES * LANES
        end = -(-(side + 1) * 2 * states // LANES) * LANES
        spans.append((begin, end))

    def second_copy(item, side, target):
        begin, end = spans[side]
        return remote(
            sums.at[item, :, pl.ds(begin, end - begin)],
            last.at[my_other],
            second_send.at[item, side],
            second_recv.at[my_other],
            owner_device(target, side),
        )

    for at in range(half):
        slot = jnp.where(parity == 0, even[at], odd[at])
        target = (z + slot) % ring
        item = target // 2
        for pos in range(line):
            arrival = remote(
                parts.at[item, pos],
                parts.at[item, pos],
                first_send.at[0, 0],
                first_recv.at[item, pos],
                line_device(pos),
            )
            pl.when(my_pos != pos)(arrival.wait_recv)
        total = parts[item, 0]
        for pos in range(1, line):
            total = total + parts[item, pos]
        sums[item] = total
        for side in range(2):
            begin, end = spans[side]
            is_self = sends_to_self & (target == x) & (side == y_hi)

            def keep_sum(item=item, begin=begin, end=end):
                last[my_other] = sums[item, :, pl.ds(begin, end - begin)]

            start(second_copy(item, side, target), jnp.logical_not(is_self))
            pl.when(is_self)(keep_sum)

    for at in range(line):
        is_self = sends_to_self & (my_other == at)
        arrival = remote(
            last.at[at], last.at[at], second_send.at[0, 0], second_recv.at[at], source_device(at)
        )
        pl.when(jnp.logical_not(is_self))(arrival.wait_recv)
    total = last[0]
    for at in range(1, line):
        total = total + last[at]
    skip = 2 * states - spans[1][0]
    gram = jnp.where(y_hi == 0, total[:, :states], total[:, skip : skip + states])
    ham = jnp.where(
        y_hi == 0, total[:, states : 2 * states], total[:, skip + states : skip + 2 * states]
    )
    out_gram[...] = gram
    out_ham[...] = ham

    for finish in unfinished:
        finish()


def per_device(ring, vectors, hblocks, coupling):
    states = vectors.shape[0]
    quarter, half, line = ring // 2, ring // 2, ring
    rows = states // quarter
    width = -(-2 * states // LANES) * LANES
    f32, bf16 = jnp.float32, jnp.bfloat16
    dma = pltpu.SemaphoreType.DMA
    gram, ham = pl.pallas_call(
        functools.partial(kernel, ring, states),
        out_shape=[jax.ShapeDtypeStruct((rows, states), f32)] * 2,
        in_specs=[
            pl.BlockSpec(memory_space=pl.ANY),
            pl.BlockSpec(memory_space=pl.ANY),
            pl.BlockSpec(memory_space=pl.ANY),
        ],
        out_specs=[pl.BlockSpec(memory_space=pltpu.VMEM)] * 2,
        scratch_shapes=[
            pltpu.SMEM((OWN, 2 * REACH), jnp.int32),
            pltpu.VMEM((OWN, 2 * REACH + 1, LANES, LANES), f32),
            pltpu.VMEM((PAIRS, 2 * LANES, WINDOW * LANES), bf16),
            pltpu.VMEM((PAIRS, 2 * LANES, WINDOW * LANES), bf16),
            pltpu.VMEM((DEGREE + 1, OWN, states, LANES), f32),
            pltpu.VMEM((DEGREE + 1, 2, REACH, states, LANES), f32),
            pltpu.VMEM((2 * states, (OWN + 2 * REACH) * LANES), bf16),
            pltpu.VMEM((PAIRS, states, 2 * LANES), f32),
            pltpu.VMEM((OWN, states, LANES), f32),
            pltpu.VMEM((ring, OWN, states, LANES), f32),
            pltpu.VMEM((OWN, states, LANES), f32),
            pltpu.VMEM((2, OWN, states, LANES), f32),
            pltpu.VMEM((4 * states, OWN * LANES), bf16),
            pltpu.VMEM((4 * states, OWN * LANES), bf16),
            pltpu.VMEM((2 * states, OWN * LANES), bf16),
            pltpu.VMEM((ring, states, 4 * states), f32),
            pltpu.VMEM((half, line, rows, 4 * states), f32),
            pltpu.VMEM((half, rows, 4 * states), f32),
            pltpu.VMEM((line, rows, width), f32),
            dma((3,)),
            dma((DEGREE + 1, 2, GROUPS)),
            dma((DEGREE + 1, 2, GROUPS)),
            dma((2, GROUPS)),
            dma((2, GROUPS)),
            dma((2, GROUPS)),
            dma((2, GROUPS)),
            dma((ring, 2)),
            dma((ring, 2)),
            dma((ring, quarter)),
            dma((half, line)),
            dma((half, 2)),
            dma((line,)),
        ],
        compiler_params=pltpu.CompilerParams(
            collective_id=0, has_side_effects=True, vmem_limit_bytes=60 * 1024 * 1024
        ),
    )(coupling, jnp.swapaxes(vectors, 0, 1), hblocks)
    return ham.T, gram.T


def solution(mesh):
    in_specs = (P("row", "col", None), P("col", None, None, None), P("col", None))
    out_specs = (P("row", "col"), P("row", "col"))
    ring = mesh.shape["row"] // 2
    return jax.shard_map(
        functools.partial(per_device, ring),
        mesh=mesh,
        in_specs=in_specs,
        out_specs=out_specs,
        check_vma=False,
    )
```

```python
import functools

import jax
import jax.numpy as jnp
from jax import lax
from jax.experimental import pallas as pl
from jax.experimental.pallas import tpu as pltpu
from jax.sharding import PartitionSpec as P

REACH = 3
DEGREE = 3

CENTER = 0.5
HALF_WIDTH = 1.5
HSCALE = 0.1

LANES = 128
OWN = 6
PAIRS = OWN // 2
WINDOW = 8
GROUPS = 2
MESH = pl.DeviceIdType.MESH


def split_high_low(value):
    high = value.astype(jnp.bfloat16)
    low = (value - high.astype(jnp.float32)).astype(jnp.bfloat16)
    return high, low


def dot_last(left, right):
    return lax.dot_general(
        left, right, (((1,), (1,)), ((), ())), preferred_element_type=jnp.float32
    )


def kernel(
    ring,
    states,
    coupling,
    vectors,
    hblocks,
    out,
    bonds,
    raw,
    band_high,
    band_low,
    fields,
    halo,
    operand,
    acc,
    image,
    blocks,
    image_block,
    sibling,
    side_high,
    side_low,
    other,
    products,
    parts,
    sums,
    last,
    load_sem,
    halo_send,
    halo_recv,
    swap_send,
    swap_recv,
    sib_send,
    sib_recv,
    ring_send,
    ring_recv,
    first_send,
    first_recv,
    second_send,
    second_recv,
):
    quarter = ring // 2
    half = ring // 2
    line = ring
    rows = states // quarter
    part = states // GROUPS

    row = lax.axis_index("row")
    col = lax.axis_index("col")
    z, y_hi = row // 2, row % 2
    x = col // (2 * quarter)
    y_lo = (col // 2) % quarter
    core = col % 2
    y = y_hi * quarter + y_lo
    last_col = ring * 2 * quarter - 1

    def device(z_at, y_at, x_at, core_at):
        return (
            z_at * 2 + y_at // quarter,
            x_at * (2 * quarter) + (y_at % quarter) * 2 + core_at,
        )

    has_low, has_high = col > 0, col < last_col
    stays = y_hi == core
    moves = y_hi != core
    my_pos = jnp.where(core == 0, y, x)
    my_other = jnp.where(core == 0, x, y)
    my_half = my_pos // quarter
    my_piece = core * quarter + my_pos % quarter
    my_out = 2 * y_lo + core
    sends_to_self = jnp.logical_and(my_piece == my_out, x % 2 == my_half)

    def line_device(pos):
        return device(z, jnp.where(core == 0, pos, y), jnp.where(core == 0, x, pos), core)

    def owner_device(target, side):
        return device(z, side * quarter + my_piece // 2, target, my_piece % 2)

    src_core = my_out // quarter
    src_pos = (my_out % quarter + quarter * x) % line

    def source_device(at):
        return device(
            z, jnp.where(src_core == 0, src_pos, at), jnp.where(src_core == 0, at, src_pos), src_core
        )

    low_device, high_device = (row, col - 1), (row, col + 1)
    swap_device = device(z, core * quarter + y_lo, x, y_hi)
    sib_device = device(z, y, x, 1 - core)
    down_device = device((z + ring - 1) % ring, y, x, core)
    up_device = device((z + 1) % ring, y, x, core)

    load = pltpu.make_async_copy(hblocks, raw, load_sem.at[0])
    load_field = pltpu.make_async_copy(vectors, fields.at[0], load_sem.at[1])
    load_bonds = pltpu.make_async_copy(coupling, bonds, load_sem.at[2])
    load_field.start()
    load_bonds.start()
    load.start()

    barrier = pltpu.get_barrier_semaphore()

    def greet(target, when=None):
        def signal():
            pl.semaphore_signal(barrier, inc=1, device_id=target, device_id_type=MESH)

        if when is None:
            signal()
        else:
            pl.when(when)(signal)

    greet(low_device, has_low)
    greet(high_device, has_high)
    greet(swap_device, moves)
    greet(sib_device)
    greet(down_device)
    greet(up_device)
    for pos in range(line):
        greet(line_device(pos), my_pos != pos)
    for item in range(half):
        target = 2 * item + my_half
        for side in range(2):
            is_self = sends_to_self & (target == x) & (side == y_hi)
            greet(owner_device(target, side), jnp.logical_not(is_self))
    for at in range(line):
        is_self = sends_to_self & (my_other == at)
        greet(source_device(at), jnp.logical_not(is_self))

    greetings = (
        has_low.astype(jnp.int32)
        + has_high.astype(jnp.int32)
        + moves.astype(jnp.int32)
        + 3
        + (line - 1)
        + 2 * half
        + line
        - 2 * sends_to_self.astype(jnp.int32)
    )
    load_field.wait()
    pl.semaphore_wait(barrier, greetings)

    unfinished = []

    def remote(src, dst, send, recv, target):
        return pltpu.make_async_remote_copy(
            src_ref=src,
            dst_ref=dst,
            send_sem=send,
            recv_sem=recv,
            device_id=target,
            device_id_type=MESH,
        )

    def start(copy, when=None):
        if when is None:
            copy.start()
            unfinished.append(copy.wait_send)
        else:
            pl.when(when)(copy.start)
            unfinished.append(lambda: pl.when(when)(copy.wait_send))

    def group_rows(g):
        return pl.ds(g * part, part)

    def halo_copy(step, side, g):
        first, target = (OWN - REACH, high_device) if side == 0 else (0, low_device)
        return remote(
            fields.at[step, pl.ds(first, REACH), group_rows(g)],
            halo.at[step, side, :, group_rows(g)],
            halo_send.at[step, side, g],
            halo_recv.at[step, side, g],
            target,
        )

    def send_halo(step, g):
        start(halo_copy(step, 0, g), has_high)
        start(halo_copy(step, 1, g), has_low)

    for g in range(GROUPS):
        send_halo(0, g)

    load_bonds.wait()
    load.wait()
    zero_block = jnp.zeros((LANES, LANES), jnp.bfloat16)
    for p in range(PAIRS):
        for band in (band_high, band_low):
            band[p, pl.ds(0, LANES), pl.ds((WINDOW - 1) * LANES, LANES)] = zero_block
            band[p, pl.ds(LANES, LANES), pl.ds(0, LANES)] = zero_block
        for second in range(2):
            a = 2 * p + second
            for o in range(2 * REACH + 1):
                scaled = HSCALE * raw[a, o]
                if o != REACH:
                    bond = bonds[a, o if o < REACH else o - 1]
                    scaled = scaled * bond.astype(jnp.float32)
                high, low = split_high_low(scaled)
                at = (pl.ds(second * LANES, LANES), pl.ds((o + second) * LANES, LANES))
                band_high[(p,) + at] = high
                band_low[(p,) + at] = low

    def put_operand(g, where, value):
        high, low = split_high_low(value)
        operand[pl.ds(2 * g * part, part), pl.ds(where * LANES, LANES)] = high
        operand[pl.ds((2 * g + 1) * part, part), pl.ds(where * LANES, LANES)] = low

    def band_product(g, p, begin, end):
        begin_row, columns = 2 * g * part, slice(begin * LANES, end * LANES)
        window = slice((begin - 2 * p) * LANES, (end - 2 * p) * LANES)
        both = dot_last(
            operand[begin_row : begin_row + 2 * part, columns], band_high[p, :, window]
        )
        rest = dot_last(operand[begin_row : begin_row + part, columns], band_low[p, :, window])
        return both[:part] + both[part:] + rest

    def clear_edge(begin):
        operand[:, pl.ds(begin * LANES, REACH * LANES)] = jnp.zeros(
            (2 * states, REACH * LANES), jnp.bfloat16
        )

    pl.when(jnp.logical_not(has_low))(lambda: clear_edge(0))
    pl.when(jnp.logical_not(has_high))(lambda: clear_edge(REACH + OWN))

    def apply_own(step, g):
        for a in range(OWN):
            put_operand(g, REACH + a, fields[step, a, group_rows(g)])
        for p in range(PAIRS):
            begin, end = max(REACH, 2 * p), min(REACH + OWN, 2 * p + WINDOW)
            acc[p, group_rows(g)] = band_product(g, p, begin, end)

    def apply_halo(step, g):
        def take(side, begin):
            halo_copy(step, side, g).wait_recv()
            for a in range(REACH):
                put_operand(g, begin + a, halo[step, side, a, group_rows(g)])

        pl.when(has_low)(lambda: take(0, 0))
        pl.when(has_high)(lambda: take(1, REACH + OWN))
        for p in range(PAIRS):
            total = acc[p, group_rows(g)]
            if 2 * p < REACH:
                total = total + band_product(g, p, 2 * p, REACH)
            if 2 * p + WINDOW > REACH + OWN:
                total = total + band_product(g, p, REACH + OWN, 2 * p + WINDOW)
            acc[p, group_rows(g)] = total

    def acted(g, a):
        return acc[a // 2, group_rows(g), pl.ds((a % 2) * LANES, LANES)]

    def ring_copy(slot, chunk):
        upward = slot > half or (slot == half and chunk == 1)
        src, target = ((slot + 1) % ring, up_device) if upward else (slot - 1, down_device)
        return remote(
            blocks.at[src, :, group_rows(chunk)],
            blocks.at[slot, :, group_rows(chunk)],
            ring_send.at[slot, chunk],
            ring_recv.at[slot, chunk],
            target,
        )

    def ring_pieces(distance):
        if distance == half:
            return [(half, 0), (half, 1)]
        return [(slot, chunk) for chunk in range(2) for slot in (distance, ring - distance)]

    def swap_copy(at, g):
        src, dst = ((fields.at[DEGREE], blocks.at[0]), (image, image_block))[at]
        return remote(
            src.at[:, group_rows(g)],
            dst.at[:, group_rows(g)],
            swap_send.at[at, g],
            swap_recv.at[at, g],
            swap_device,
        )

    def sib_copy(at, g):
        src = (blocks.at[0], image_block)[at]
        return remote(
            src.at[:, group_rows(g)],
            sibling.at[at, :, group_rows(g)],
            sib_send.at[at, g],
            sib_recv.at[at, g],
            sib_device,
        )

    def forward(distance):
        for slot, chunk in ring_pieces(distance):
            ring_copy(slot, chunk).wait_recv()
            if distance < half:
                beyond = slot + 1 if slot < half else slot - 1
                if beyond != half or chunk == (0 if slot < half else 1):
                    ring_copy(beyond, chunk).start()

    def begin_ring(g):
        for slot, chunk in ring_pieces(1):
            if chunk == g:
                ring_copy(slot, chunk).start()
        sib_copy(0, g).start()

    for distance in range(1, half + 1):
        for piece in ring_pieces(distance):
            unfinished.append(ring_copy(*piece).wait_send)
    for at in range(2):
        for g in range(GROUPS):
            unfinished.append(sib_copy(at, g).wait_send)

    def keep_field(g):
        blocks[0, :, group_rows(g)] = fields[DEGREE, :, group_rows(g)]
        begin_ring(g)

    def take_field():
        for g in range(GROUPS):
            swap_copy(0, g).wait_recv()
            begin_ring(g)

    def keep_image(g):
        image_block[:, group_rows(g)] = image[:, group_rows(g)]
        sib_copy(1, g).start()

    def take_image():
        for g in range(GROUPS):
            swap_copy(1, g).wait_recv()
            sib_copy(1, g).start()

    def put_side(begin, source):
        for a in range(OWN):
            high, low = split_high_low(source(a))
            at = (pl.ds(begin, states), pl.ds(a * LANES, LANES))
            side_high[at] = high
            side_low[at] = low

    own_rows = pl.multiple_of(core * (2 * states), 2 * states)
    sib_rows = pl.multiple_of((1 - core) * (2 * states), 2 * states)

    for step in range(DEGREE):
        for g in range(GROUPS):
            apply_own(step, g)
            apply_halo(step, g)
            for a in range(OWN):
                now = fields[step, a, group_rows(g)]
                if step == 0:
                    later = (acted(g, a) - CENTER * now) / HALF_WIDTH
                else:
                    before = fields[step - 1, a, group_rows(g)]
                    later = 2.0 * (acted(g, a) - CENTER * now) / HALF_WIDTH - before
                fields[step + 1, a, group_rows(g)] = later
            send_halo(step + 1, g)
            if step == DEGREE - 1:
                start(swap_copy(0, g), moves)
                pl.when(stays)(functools.partial(keep_field, g))

    for g in range(GROUPS):
        apply_own(DEGREE, g)
        apply_halo(DEGREE, g)
        for a in range(OWN):
            image[a, group_rows(g)] = acted(g, a)
        start(swap_copy(1, g), moves)
        pl.when(stays)(functools.partial(keep_image, g))
        if g == 0:
            pl.when(stays)(lambda: forward(1))
    pl.when(moves)(take_field)
    if half > 1:
        pl.when(stays)(lambda: forward(2))
    put_side(own_rows, lambda a: blocks[0, a])
    for g in range(GROUPS):
        sib_copy(0, g).wait_recv()
    put_side(sib_rows, lambda a: sibling[0, a])
    pl.when(moves)(take_image)
    for distance in range(3, half + 1):
        pl.when(stays)(functools.partial(forward, distance))
    put_side(own_rows + states, lambda a: image_block[a])
    for g in range(GROUPS):
        sib_copy(1, g).wait_recv()
    put_side(sib_rows + states, lambda a: sibling[1, a])

    def first_copy(slot, piece):
        target = (z + slot) % ring
        pos = (piece + quarter * target) % line
        copy = remote(
            products.at[slot, pl.ds(piece * rows, rows)],
            parts.at[target // 2, my_pos],
            first_send.at[slot, piece],
            first_recv.at[target // 2, my_pos],
            line_device(pos),
        )
        return copy, pos, target // 2

    def multiply(slot):
        for a in range(OWN):
            high, low = split_high_low(blocks[slot, a])
            other[pl.ds(0, states), pl.ds(a * LANES, LANES)] = high
            other[pl.ds(states, states), pl.ds(a * LANES, LANES)] = low
        both = dot_last(other[...], side_high[...])
        rest = dot_last(other[:states], side_low[...])
        products[slot] = both[:states] + both[states:] + rest
        for piece in range(quarter):
            copy, pos, item = first_copy(slot, piece)

            def keep(item=item, piece=piece):
                parts[item, my_pos] = products[slot, pl.ds(piece * rows, rows), :]

            start(copy, pos != my_pos)
            pl.when(pos == my_pos)(keep)

    multiply(0)
    pl.when(moves)(lambda: forward(1))
    for distance in range(1, half + 1):
        if distance > 1:
            pl.when(moves)(functools.partial(forward, distance))
        multiply(distance)
        if distance != half:
            multiply(ring - distance)

    order = sorted(range(ring), key=lambda d: (min(d, ring - d), d))
    even = [d for d in order if d % 2 == 0]
    odd = [d for d in order if d % 2 == 1]
    parity = (z + my_half) % 2
    spans = []
    for side in range(2):
        begin = side * 2 * states // LANES * LANES
        end = -(-(side + 1) * 2 * states // LANES) * LANES
        spans.append((begin, end))

    def second_copy(item, side, target):
        begin, end = spans[side]
        return remote(
            sums.at[item, :, pl.ds(begin, end - begin)],
            last.at[my_other],
            second_send.at[item, side],
            second_recv.at[my_other],
            owner_device(target, side),
        )

    for at in range(half):
        slot = jnp.where(parity == 0, even[at], odd[at])
        target = (z + slot) % ring
        item = target // 2
        for pos in range(line):
            arrival = remote(
                parts.at[item, pos],
                parts.at[item, pos],
                first_send.at[0, 0],
                first_recv.at[item, pos],
                line_device(pos),
            )
            pl.when(my_pos != pos)(arrival.wait_recv)
        total = parts[item, 0]
        for pos in range(1, line):
            total = total + parts[item, pos]
        sums[item] = total
        for side in range(2):
            begin, end = spans[side]
            is_self = sends_to_self & (target == x) & (side == y_hi)

            def keep_sum(item=item, begin=begin, end=end):
                last[my_other] = sums[item, :, pl.ds(begin, end - begin)]

            start(second_copy(item, side, target), jnp.logical_not(is_self))
            pl.when(is_self)(keep_sum)

    for at in range(line):
        is_self = sends_to_self & (my_other == at)
        arrival = remote(
            last.at[at], last.at[at], second_send.at[0, 0], second_recv.at[at], source_device(at)
        )
        pl.when(jnp.logical_not(is_self))(arrival.wait_recv)
    total = last[0]
    for at in range(1, line):
        total = total + last[at]
    skip = 2 * states - spans[1][0]
    gram = jnp.where(y_hi == 0, total[:, :states], total[:, skip : skip + states])
    ham = jnp.where(
        y_hi == 0, total[:, states : 2 * states], total[:, skip + states : skip + 2 * states]
    )
    out[0] = ham
    out[1] = gram

    for finish in unfinished:
        finish()


def per_device(ring, vectors, hblocks, coupling):
    states = vectors.shape[0]
    quarter, half, line = ring // 2, ring // 2, ring
    rows = states // quarter
    width = -(-2 * states // LANES) * LANES
    f32, bf16 = jnp.float32, jnp.bfloat16
    dma = pltpu.SemaphoreType.DMA
    both = pl.pallas_call(
        functools.partial(kernel, ring, states),
        out_shape=jax.ShapeDtypeStruct((2, rows, states), f32),
        in_specs=[
            pl.BlockSpec(memory_space=pl.ANY),
            pl.BlockSpec(memory_space=pl.ANY),
            pl.BlockSpec(memory_space=pl.ANY),
        ],
        out_specs=pl.BlockSpec(memory_space=pltpu.VMEM),
        scratch_shapes=[
            pltpu.SMEM((OWN, 2 * REACH), jnp.int32),
            pltpu.VMEM((OWN, 2 * REACH + 1, LANES, LANES), f32),
            pltpu.VMEM((PAIRS, 2 * LANES, WINDOW * LANES), bf16),
            pltpu.VMEM((PAIRS, 2 * LANES, WINDOW * LANES), bf16),
            pltpu.VMEM((DEGREE + 1, OWN, states, LANES), f32),
            pltpu.VMEM((DEGREE + 1, 2, REACH, states, LANES), f32),
            pltpu.VMEM((2 * states, (OWN + 2 * REACH) * LANES), bf16),
            pltpu.VMEM((PAIRS, states, 2 * LANES), f32),
            pltpu.VMEM((OWN, states, LANES), f32),
            pltpu.VMEM((ring, OWN, states, LANES), f32),
            pltpu.VMEM((OWN, states, LANES), f32),
            pltpu.VMEM((2, OWN, states, LANES), f32),
            pltpu.VMEM((4 * states, OWN * LANES), bf16),
            pltpu.VMEM((4 * states, OWN * LANES), bf16),
            pltpu.VMEM((2 * states, OWN * LANES), bf16),
            pltpu.VMEM((ring, states, 4 * states), f32),
            pltpu.VMEM((half, line, rows, 4 * states), f32),
            pltpu.VMEM((half, rows, 4 * states), f32),
            pltpu.VMEM((line, rows, width), f32),
            dma((3,)),
            dma((DEGREE + 1, 2, GROUPS)),
            dma((DEGREE + 1, 2, GROUPS)),
            dma((2, GROUPS)),
            dma((2, GROUPS)),
            dma((2, GROUPS)),
            dma((2, GROUPS)),
            dma((ring, 2)),
            dma((ring, 2)),
            dma((ring, quarter)),
            dma((half, line)),
            dma((half, 2)),
            dma((line,)),
        ],
        compiler_params=pltpu.CompilerParams(
            collective_id=0, has_side_effects=True, vmem_limit_bytes=60 * 1024 * 1024
        ),
    )(coupling, jnp.swapaxes(vectors, 0, 1), hblocks)
    return both[0].T, both[1].T


def solution(mesh):
    in_specs = (P("row", "col", None), P("col", None, None, None), P("col", None))
    out_specs = (P("row", "col"), P("row", "col"))
    ring = mesh.shape["row"] // 2
    return jax.shard_map(
        functools.partial(per_device, ring),
        mesh=mesh,
        in_specs=in_specs,
        out_specs=out_specs,
        check_vma=False,
    )
```
